512 devices in a mesh: ctx: 128 (over z, x, core), dec: 4 (over y).
Axes of the slice: x: 4, y: 4, z: 16, core: 2. Of those that a mesh axis runs over, the one named last changes fastest.
Arguments:
- frames: bfloat16 [65536, 1280], P('ctx', 'dec'), may hold values from -20 to 20
- queries: bfloat16 [16384, 1280], P('ctx', 'dec'), may hold values from -128 to 128
- align_start: int32 [512], P('ctx'), may hold values from 0 to 2047, as said below
- align_end: int32 [512], P('ctx'), may hold values from 1 to 2048
- gain_conv: float32 [1280], P('dec'), may hold values from 0.25 to 1.75
- conv_kernel: float32 [31, 1280], P(None, 'dec'), may hold values from -1 to 1
- gain_attn: float32 [1280], P('dec'), may hold values from 0.25 to 1.75
- w_qkv: bfloat16 [1280, 3, 1280], P(None, None, 'dec'), may hold values from -3 to 3
- w_out: bfloat16 [1280, 1280], P(None, 'dec'), may hold values from -0.625 to 0.625
Outputs:
- encoded: bfloat16 [65536, 1280], P('ctx', 'dec')
- crossed: bfloat16 [16384, 1280], P('ctx', 'dec')
The draws below stay inside these ranges and needn't reach their ends.
Inputs may be any that keep to these rules, and one draw needn't show every extreme that they name: Token blocks on ctx index c read only frame blocks of ctx indices c-1, c and c+1; align_end - align_start lies between 1 and 8 and equals 8 for the first token block of each ctx index.
All inputs are finite; a program needn't handle non-finite values.
Results may differ from the reference program's by a relative error of at most 0.029.
The reference program's roundings to bfloat16 on the way count: a program that leaves them out, or rounds other values in their place, can miss the bound.
Values may be sent and summed in bfloat16 or wider, within the bound.
No kernel may reach another device: no remote copies, remote signals or barrier semaphores. Data moves between devices by JAX's collectives and lax.ppermute only.
A program may use at most 64 MiB of HBM per device.

```python
import jax
import jax.numpy as jnp
from jax import lax

HEADS = 20
HD = 64
D = 1280
KW = 31
WIN = 1024
FB = 32
SPAN_BLK = 8
TB = 32
F_DEV = 512
TOK_DEV = 128
FRAMES = 65536
TOKENS = 16384


def alignment_lists(key):
    per_dev = TOK_DEV // TB
    frame_blocks = F_DEV // FB
    total_blocks = FRAMES // FB
    ids = jnp.arange(TOKENS // TB, dtype=jnp.int32)
    owner = ids // per_dev
    local = ids % per_dev
    key_len, key_off = jax.random.split(key)
    length = jax.random.randint(key_len, ids.shape, 1, SPAN_BLK + 1)
    length = jnp.where(local == 0, SPAN_BLK, length)
    offset = jax.random.randint(key_off, ids.shape, -frame_blocks, frame_blocks + 1)
    base = owner * frame_blocks + local * frame_blocks // per_dev + offset
    lowest = jnp.maximum((owner - 1) * frame_blocks, 0)
    highest = jnp.minimum((owner + 2) * frame_blocks, total_blocks) - length
    start = jnp.minimum(jnp.maximum(base, lowest), highest)
    return (start.astype(jnp.int32), (start + length).astype(jnp.int32))


def draw_align_start(key, part):
    return alignment_lists(key)[0]


def draw_align_end(key, part):
    return alignment_lists(key)[1]


def draw_frames(key, part):
    key = jax.random.fold_in(key, 5)
    place = jnp.arange(D, dtype=jnp.float32) / D
    values = jnp.clip(jax.random.normal(key, (FRAMES, D), jnp.float32), -6.0, 6.0)
    column = jnp.exp((place - 0.5) * 2.3025851)
    return (values * column[None, :]).astype(jnp.bfloat16)


def draw_queries(key, part):
    key = jax.random.fold_in(key, 7)
    key_val = jax.random.fold_in(key, 0)
    result = jnp.clip(jax.random.normal(key_val, (TOKENS, D), jnp.float32), -6.0, 6.0)
    return result.astype(jnp.bfloat16)


def draw_w_qkv(key, part):
    key = jax.random.fold_in(key, 11)
    key_val = jax.random.fold_in(key, 0)
    result = jnp.clip(jax.random.normal(key_val, (D, 3, D), jnp.float32), -4.0, 4.0) * D ** (-0.5)
    return result.astype(jnp.bfloat16)


def levels(rng, extent, cuts, low, top_value):
    factor_of = 1.0
    for position, blocks in cuts:
        draws = jax.random.uniform(jax.random.fold_in(jax.random.fold_in(rng, 6), position), (blocks,), jnp.float32, low / len(cuts), top_value / len(cuts))
        factor_of = factor_of * jnp.repeat(jnp.exp(draws), extent[position] // blocks).reshape((-1,) + (1,) * (len(extent) - 1 - position))
    return factor_of


def scatter_about(stream_key, shape, deviation, most, shards=(), held_as=jnp.bfloat16):
    array = deviation * jax.random.normal(stream_key, shape, jnp.float32)
    if shards:
        array = array * levels(stream_key, shape, shards, -0.22, 0.18)
    return jnp.clip(array, -most, most).astype(held_as)


def setup_inputs(seed: int = 0) -> dict:
    key_list = jax.random.split(jax.random.key(seed), 10)
    return {
        "frames": draw_frames(jax.random.fold_in(key_list[9], 71), 0),
        "queries": draw_queries(jax.random.fold_in(key_list[9], 71), 0),
        "align_start": draw_align_start(jax.random.fold_in(key_list[9], 71), 0),
        "align_end": draw_align_end(jax.random.fold_in(key_list[9], 71), 0),
        "gain_conv": jnp.clip(1.0 + 0.15 * jax.random.normal(key_list[4], (D,), jnp.float32), 0.25, 1.75),
        "conv_kernel": scatter_about(key_list[5], (KW, D), KW ** -0.5, 1.0, ((1, 4),), jnp.float32),
        "gain_attn": jnp.clip(1.0 + 0.15 * jax.random.normal(key_list[6], (D,), jnp.float32), 0.25, 1.75),
        "w_qkv": draw_w_qkv(jax.random.fold_in(key_list[9], 71), 0),
        "w_out": scatter_about(key_list[8], (D, D), (D // 16) ** -0.5, 0.625, ((1, 4),)),
    }


def rms_rows(values, gain):
    mean_sq = lax.optimization_barrier(jnp.mean(values * values, axis=1, keepdims=True))
    return values * lax.rsqrt(mean_sq + 1e-06) * gain

def masked_softmax(scores, keep):
    scores = jnp.where(keep, scores, -jnp.inf)
    peak = lax.optimization_barrier(jnp.max(scores, axis=-1, keepdims=True))
    expo = jnp.exp(scores - peak)
    return expo / lax.optimization_barrier(jnp.sum(expo, axis=-1, keepdims=True))

def reference(frames, queries, align_start, align_end, gain_conv, conv_kernel, gain_attn, w_qkv, w_out):
    scale = HD ** (-0.5)
    x_float = frames.astype(jnp.float32)
    normed = rms_rows(x_float, gain_conv).astype(jnp.bfloat16)
    half = (KW - 1) // 2
    padded = jnp.pad(normed, ((half, half), (0, 0)))
    conv = jnp.zeros((FRAMES, D), jnp.float32)
    for tap in range(KW):
        conv = conv + padded[tap:tap + FRAMES].astype(jnp.float32) * conv_kernel[tap]
    resid = x_float + jax.nn.silu(conv)
    normed2 = rms_rows(resid, gain_attn).astype(jnp.bfloat16)
    proj = jnp.dot(normed2, w_qkv.reshape(D, 3 * D), preferred_element_type=jnp.float32)
    q_all = proj[:, :D].astype(jnp.bfloat16)
    k_all = proj[:, D:2 * D].astype(jnp.bfloat16)
    v_all = proj[:, 2 * D:].astype(jnp.bfloat16)
    qrows = min(512, F_DEV)
    k_pad = jnp.pad(k_all, ((WIN, 0), (0, 0)))
    v_pad = jnp.pad(v_all, ((WIN, 0), (0, 0)))

    def enc_block(index):
        first = (index * qrows).astype(jnp.int32)
        q_blk = lax.dynamic_slice_in_dim(q_all, first, qrows, 0).reshape(qrows, HEADS, HD).astype(jnp.float32)
        k_blk = lax.dynamic_slice_in_dim(k_pad, first, WIN + qrows, 0).reshape(WIN + qrows, HEADS, HD).astype(jnp.float32)
        v_blk = lax.dynamic_slice_in_dim(v_pad, first, WIN + qrows, 0).reshape(WIN + qrows, HEADS, HD).astype(jnp.float32)
        scores = jnp.einsum('qhd,khd->hqk', q_blk, k_blk) * scale
        qpos = first + jnp.arange(qrows, dtype=jnp.int32)
        kpos = first - WIN + jnp.arange(WIN + qrows, dtype=jnp.int32)
        keep = (kpos[None, :] <= qpos[:, None]) & (kpos[None, :] > qpos[:, None] - WIN) & (kpos[None, :] >= 0)
        probs = masked_softmax(scores, keep[None]).astype(jnp.bfloat16)
        out = jnp.einsum('hqk,khd->qhd', probs.astype(jnp.float32), v_blk)
        return out.reshape(qrows, D).astype(jnp.bfloat16)
    attn = lax.map(enc_block, jnp.arange(FRAMES // qrows, dtype=jnp.int32)).reshape(FRAMES, D)
    encoded = (resid + jnp.dot(attn, w_out, preferred_element_type=jnp.float32)).astype(jnp.bfloat16)
    span = SPAN_BLK * FB
    q_blocks = queries.reshape(TOKENS // TB, TB, HEADS, HD)

    def cross_block(items):
        q_blk, first_blk, end_blk = items
        first = jnp.clip(first_blk * FB, 0, FRAMES - span).astype(jnp.int32)
        k_win = lax.dynamic_slice_in_dim(k_all, first, span, 0).reshape(span, HEADS, HD).astype(jnp.float32)
        v_win = lax.dynamic_slice_in_dim(v_all, first, span, 0).reshape(span, HEADS, HD).astype(jnp.float32)
        scores = jnp.einsum('qhd,khd->hqk', q_blk.astype(jnp.float32), k_win) * scale
        kpos = first + jnp.arange(span, dtype=jnp.int32)
        keep = (kpos >= first_blk * FB) & (kpos < end_blk * FB)
        probs = masked_softmax(scores, keep[None, None, :]).astype(jnp.bfloat16)
        out = jnp.einsum('hqk,khd->qhd', probs.astype(jnp.float32), v_win)
        return out.reshape(TB, D).astype(jnp.bfloat16)
    crossed = lax.map(cross_block, (q_blocks, align_start, align_end)).reshape(TOKENS, D)
    return (encoded, crossed)
```

```python
import functools

import jax
import jax.numpy as jnp
from jax import lax
from jax.experimental import pallas as pl
from jax.experimental.pallas import tpu as pltpu
from jax.sharding import PartitionSpec as P

HD = 64
D = 1280
WIN = 1024
FB = 32
TB = 32
KW = 31
HALF = 15
EPS = 1e-06
SCALE = HD ** (-0.5)
LOG2E = 1.4426950408889634
FAR = 1e30
RIM = 16
LANES = 128

VMEM = pl.BlockSpec(memory_space=pltpu.VMEM)
SMEM = pl.BlockSpec(memory_space=pltpu.SMEM)
HBM = pl.BlockSpec(memory_space=pltpu.HBM)


def call(kernel, outs, smem, operands, scratch=(), hbm=0, mib=16, flops=0, nbytes=0, exps=0):
    specs = [SMEM] * smem + [VMEM] * (len(operands) - smem - hbm) + [HBM] * hbm
    return pl.pallas_call(
        kernel,
        out_shape=outs,
        in_specs=specs,
        out_specs=jax.tree.map(lambda _: VMEM, outs),
        scratch_shapes=list(scratch),
        compiler_params=pltpu.CompilerParams(vmem_limit_bytes=mib * 1024 * 1024),
        cost_estimate=pl.CostEstimate(flops=flops, bytes_accessed=nbytes, transcendentals=exps),
    )(*operands)


def rot(block, axis, distance):
    count = lax.axis_size(axis)
    return lax.ppermute(block, axis, [(i, (i + distance) % count) for i in range(count)])


def shifted(block, axis, distance):
    devices = range(lax.axis_size(axis))
    return lax.ppermute(block, axis, [(i, i + distance) for i in devices if i + distance in devices])


def pack_body(left_ref, right_ref, taps_ref, gain1_ref, gain2_ref, out_ref):
    out_ref[0:RIM, :] = left_ref[...].astype(jnp.float32)
    out_ref[RIM : 2 * RIM, :] = right_ref[...].astype(jnp.float32)
    out_ref[2 * RIM : 2 * RIM + KW, :] = taps_ref[...]
    out_ref[2 * RIM + KW : 2 * RIM + KW + 1, :] = gain1_ref[...]
    out_ref[2 * RIM + KW + 1 : 2 * RIM + KW + 2, :] = gain2_ref[...]
    out_ref[2 * RIM + KW + 2 :, :] = jnp.zeros((7, out_ref.shape[1]), jnp.float32)


def hold_body(in_ref, out_ref, sem):
    copy = pltpu.make_async_copy(in_ref, out_ref, sem)
    copy.start()
    copy.wait()


def place(dec, blocks, whole_ref, width):
    for offset, block in blocks:
        at = pl.multiple_of(lax.rem(dec + offset, 4) * width, width)
        whole_ref[pl.ds(at, width), :] = block[:width, :]


def rounded(value):
    return value.astype(jnp.bfloat16).astype(jnp.float32)


def front_body(
    dec_ref, own_ref, b1_ref, b2_ref, b3_ref, pay_ref, w_ref, q_ref, kv_ref, resid_ref,
    xall_ref, x_ref, pad_ref, scale_ref, square_ref, whole_ref, turned_ref, norm_ref,
):
    width, rows = own_ref.shape
    dec = dec_ref[0]
    place(dec, [(0, own_ref), (3, b1_ref), (2, b2_ref), (1, b3_ref)], xall_ref, width)
    tiles = D // LANES

    def gather_square(f, total):
        at = pl.ds(pl.multiple_of(f * LANES, LANES), LANES)
        x = xall_ref[at, :].astype(jnp.float32)
        return total + jnp.sum((x * x).reshape(LANES // 8, 8, rows), axis=0)

    total = lax.fori_loop(0, tiles, gather_square, jnp.zeros((8, rows), jnp.float32))
    scale = lax.rsqrt(jnp.sum(total, axis=0, keepdims=True) / D + EPS)
    scale_ref[...] = jnp.broadcast_to(scale, (LANES, rows)).T
    rims = pay_ref[0 : 2 * RIM, :]
    rim_scale = lax.rsqrt(jnp.sum(rims * rims, axis=1, keepdims=True) / D + EPS)
    square_ref[...] = jnp.zeros_like(square_ref)
    strip = 64

    def tile(f, carry):
        lanes = pl.ds(pl.multiple_of(f * LANES, LANES), LANES)
        gain = pay_ref[2 * RIM + KW : 2 * RIM + KW + 1, lanes]
        x_ref[...] = xall_ref[lanes, :].astype(jnp.float32).T
        rim = rounded(pay_ref[0 : 2 * RIM, lanes] * rim_scale * gain)
        pad_ref[0:RIM, :] = rim[:RIM]
        pad_ref[RIM + rows : 2 * RIM + rows, :] = rim[RIM:]
        pad_ref[RIM : RIM + rows, :] = rounded(x_ref[...] * scale_ref[...] * gain)
        for t in range(0, rows, strip):
            conv = None
            for b in range(8):
                moved = pad_ref[t + b + 1 : t + b + 1 + strip + 24, :]
                for a in range(4):
                    tap = 8 * a + b
                    if tap < KW:
                        k = pay_ref[2 * RIM + tap : 2 * RIM + tap + 1, lanes]
                        term = moved[8 * a : 8 * a + strip] * k
                        conv = term if conv is None else conv + term
            resid = x_ref[t : t + strip, :] + conv / (1.0 + jnp.exp(-conv))
            whole_ref[f, t : t + strip, :] = resid
            square_ref[t : t + strip, :] += resid * resid

        @pl.when((f * LANES < (dec + 1) * width) & ((f + 1) * LANES > dec * width))
        def _():
            turned_ref[lanes, :] = whole_ref[f].T

        return carry

    lax.fori_loop(0, tiles, tile, 0)
    resid_ref[...] = turned_ref[pl.ds(pl.multiple_of(dec * width, HD), width), :]
    scale2 = lax.rsqrt(jnp.sum(square_ref[...], axis=1, keepdims=True) / D + EPS)
    for f in range(tiles):
        lanes = slice(f * LANES, (f + 1) * LANES)
        gain = pay_ref[2 * RIM + KW + 1 : 2 * RIM + KW + 2, lanes]
        norm_ref[:, lanes] = (whole_ref[f] * scale2 * gain).astype(jnp.bfloat16)
    for third in (1, 2, 0):
        proj = lax.dot_general(
            w_ref[third * width : (third + 1) * width, :],
            norm_ref[...],
            (((1,), (1,)), ((), ())),
            preferred_element_type=jnp.float32,
        ).astype(jnp.bfloat16)
        if third == 0:
            q_ref[...] = proj * jnp.bfloat16(SCALE)
        else:
            kv_ref[(third - 1) * width : third * width, :] = proj


def tdot(left, right):
    return lax.dot_general(left, right, (((0,), (0,)), ((), ())), preferred_element_type=jnp.float32)


def self_body(pos_ref, q_ref, own_ref, left_ref, far_ref, out_ref):
    width, rows = q_ref.shape
    tile = rows // 2
    pos = pos_ref[0]
    has_left = pos >= 1
    has_far = pos >= 2
    j = lax.broadcasted_iota(jnp.int32, (tile, tile), 0)
    i = lax.broadcasted_iota(jnp.int32, (tile, tile), 1)
    after = j > i

    def head(h, carry):
        at = pl.ds(pl.multiple_of(h * HD, HD), HD)
        vt = pl.ds(pl.multiple_of(width + h * HD, HD), HD)
        for part in range(2):
            cols = slice(part * tile, (part + 1) * tile)
            q = q_ref[at, cols]
            pieces = [(far_ref, part * tile, (part + 1) * tile, has_far, 1)]
            if part == 0:
                pieces.append((far_ref, tile, rows, has_far, 0))
            pieces.append((left_ref, 0, rows, has_left, 0))
            if part == 1:
                pieces.append((own_ref, 0, tile, None, 0))
            pieces.append((own_ref, part * tile, (part + 1) * tile, None, 2))
            scores = []
            peak = None
            for ref, lo, hi, present, mask in pieces:
                s = tdot(ref[at, lo:hi], q)
                if mask == 1:
                    s = jnp.where(after, s, -FAR)
                elif mask == 2:
                    s = jnp.where(after, -FAR, s)
                top = jnp.max(s, axis=0, keepdims=True)
                if present is not None:
                    top = jnp.where(present, top, -FAR)
                peak = top if peak is None else jnp.maximum(peak, top)
                scores.append(s)
            peak = peak * LOG2E
            total = None
            acc = None
            for (ref, lo, hi, present, mask), s in zip(pieces, scores):
                less = peak if present is None else jnp.where(present, peak, FAR)
                p = jnp.exp2(s * LOG2E - less)
                add = jnp.sum(p, axis=0, keepdims=True)
                total = add if total is None else total + add
                o = jnp.dot(ref[vt, lo:hi], p.astype(jnp.bfloat16), preferred_element_type=jnp.float32)
                acc = o if acc is None else acc + o
            out_ref[at, cols] = (acc / total).astype(jnp.bfloat16)
        return carry

    lax.fori_loop(0, width // HD, head, 0)


def cross_body(pos_ref, q_ref, ends_ref, left_ref, own_ref, right_ref, out_ref):
    width, tokens = q_ref.shape
    rows = own_ref.shape[1]
    first = ends_ref[0:1, :]
    last = ends_ref[1:2, :]
    base = (pos_ref[0] - 1) * rows
    refs = (left_ref, own_ref, right_ref)
    keeps = []
    for n in range(3):
        kpos = lax.broadcasted_iota(jnp.int32, (rows, tokens), 0) + (base + n * rows)
        keeps.append((kpos >= first) & (kpos < last))

    for h in range(width // HD):
        at = slice(h * HD, (h + 1) * HD)
        vt = slice(width + h * HD, width + (h + 1) * HD)
        q = q_ref[at, :] * jnp.bfloat16(SCALE)
        scores = [jnp.where(keep, tdot(ref[at, :], q), -FAR) for ref, keep in zip(refs, keeps)]
        peak = functools.reduce(jnp.maximum, [jnp.max(s, axis=0, keepdims=True) for s in scores]) * LOG2E
        total = None
        acc = None
        for ref, s in zip(refs, scores):
            p = jnp.exp2(s * LOG2E - peak)
            add = jnp.sum(p, axis=0, keepdims=True)
            total = add if total is None else total + add
            o = jnp.dot(ref[vt, :], p.astype(jnp.bfloat16), preferred_element_type=jnp.float32)
            acc = o if acc is None else acc + o
        out_ref[at, :] = (acc / total).astype(jnp.bfloat16)


def out_body(dec_ref, own_ref, b1_ref, b2_ref, b3_ref, w_ref, resid_ref, out_ref, whole_ref):
    width = own_ref.shape[0]
    place(dec_ref[0], [(0, own_ref), (3, b1_ref), (2, b2_ref), (1, b3_ref)], whole_ref, width)
    mixed = jnp.dot(w_ref[...], whole_ref[...], preferred_element_type=jnp.float32)
    out_ref[...] = (resid_ref[...] + mixed).astype(jnp.bfloat16)


def local(frames, queries, align_start, align_end, gain_conv, conv_kernel, gain_attn, w_qkv, w_out):
    bf16, f32 = jnp.bfloat16, jnp.float32
    x = frames.T
    width, rows = x.shape
    tokens = queries.shape[0]
    dec = lax.axis_index("dec").astype(jnp.int32).reshape(1)
    pos = lax.axis_index("ctx").astype(jnp.int32).reshape(1)
    sds = jax.ShapeDtypeStruct

    b2, b1, b3 = rot(x, "dec", 2), rot(x, "dec", 1), rot(x, "dec", 3)
    from_left = shifted(frames[rows - RIM :], "ctx", 1)
    from_right = shifted(frames[:RIM], "ctx", -1)
    pay = call(
        pack_body,
        sds((72, width), f32),
        0,
        (from_left, from_right, conv_kernel, gain_conv[None], gain_attn[None]),
        mib=4,
        flops=50_000_000_000,
        nbytes=300_000,
    )
    pay = lax.all_gather(pay, "dec", axis=1, tiled=True)
    w_t = jnp.transpose(w_qkv, (1, 2, 0)).reshape(3 * width, D)
    w_t = call(hold_body, sds(w_t.shape, bf16), 0, (w_t,), hbm=1, mib=4, scratch=[pltpu.SemaphoreType.DMA], nbytes=5_000_000)
    wo_t = w_out.T
    ends = jnp.stack([jnp.repeat(align_start * FB, TB), jnp.repeat(align_end * FB, TB)], 0)
    ends = jnp.concatenate([ends, jnp.zeros((6, tokens), jnp.int32)], axis=0)

    q, kv, resid = call(
        front_body,
        (sds((width, rows), bf16), sds((2 * width, rows), bf16), sds((width, rows), f32)),
        1,
        (dec, x, b1, b2, b3, pay, w_t),
        mib=20,
        scratch=[
            pltpu.VMEM((D, rows), bf16),
            pltpu.VMEM((rows, LANES), f32),
            pltpu.VMEM((rows + 3 * RIM, LANES), f32),
            pltpu.VMEM((rows, LANES), f32),
            pltpu.VMEM((rows, LANES), f32),
            pltpu.VMEM((D // LANES, rows, LANES), f32),
            pltpu.VMEM((D, rows), f32),
            pltpu.VMEM((rows, D), bf16),
        ],
        flops=2 * 3 * width * D * rows,
        nbytes=5_000_000,
    )
    far = shifted(kv, "ctx", 2)
    left = shifted(kv, "ctx", 1)
    right = shifted(kv, "ctx", -1)
    attn = call(
        self_body,
        sds((width, rows), bf16),
        1,
        (pos, q, kv, left, far),
        flops=8 * width * rows * 1280,
        nbytes=2_500_000,
        exps=5 * rows * 1280,
    )
    a2, a1, a3 = rot(attn, "dec", 2), rot(attn, "dec", 1), rot(attn, "dec", 3)
    crossed = call(
        cross_body,
        sds((width, tokens), bf16),
        1,
        (pos, queries.T, ends, left, kv, right),
        flops=4 * width * tokens * 3 * rows,
        nbytes=2_000_000,
        exps=5 * tokens * 3 * rows,
    )
    encoded = call(
        out_body,
        sds((width, rows), bf16),
        1,
        (dec, attn, a1, a2, a3, wo_t, resid),
        scratch=[pltpu.VMEM((D, rows), bf16)],
        flops=2 * width * D * rows,
        nbytes=3_500_000,
    )
    return (encoded.T, crossed.T)


def solution(mesh):
    placed = (
        P("ctx", "dec"),
        P("ctx", "dec"),
        P("ctx"),
        P("ctx"),
        P("dec"),
        P(None, "dec"),
        P("dec"),
        P(None, None, "dec"),
        P(None, "dec"),
    )
    return jax.shard_map(
        local,
        mesh=mesh,
        in_specs=placed,
        out_specs=(P("ctx", "dec"), P("ctx", "dec")),
        check_vma=False,
    )
```

```python
import functools

import jax
import jax.numpy as jnp
from jax import lax
from jax.experimental import pallas as pl
from jax.experimental.pallas import tpu as pltpu
from jax.sharding import PartitionSpec as P

HD = 64
D = 1280
WIN = 1024
FB = 32
TB = 32
KW = 31
HALF = 15
EPS = 1e-06
SCALE = HD ** (-0.5)
LOG2E = 1.4426950408889634
FAR = 1e30
RIM = 16
LANES = 128

VMEM = pl.BlockSpec(memory_space=pltpu.VMEM)
SMEM = pl.BlockSpec(memory_space=pltpu.SMEM)
HBM = pl.BlockSpec(memory_space=pltpu.HBM)


def call(kernel, outs, smem, operands, scratch=(), hbm=0, mib=32, flops=0, nbytes=0, exps=0):
    specs = [SMEM] * smem + [VMEM] * (len(operands) - smem - hbm) + [HBM] * hbm
    return pl.pallas_call(
        kernel,
        out_shape=outs,
        in_specs=specs,
        out_specs=jax.tree.map(lambda _: VMEM, outs),
        scratch_shapes=list(scratch),
        compiler_params=pltpu.CompilerParams(vmem_limit_bytes=mib * 1024 * 1024),
        cost_estimate=pl.CostEstimate(flops=flops, bytes_accessed=nbytes, transcendentals=exps),
    )(*operands)


def swapped(block, axis, bits):
    return lax.ppermute(block, axis, [(i, i ^ bits) for i in range(lax.axis_size(axis))])


def across(block, axis):
    pairs = range(1, lax.axis_size(axis) - 1, 2)
    return lax.ppermute(block, axis, [(i, i + 1) for i in pairs] + [(i + 1, i) for i in pairs])


def shifted(block, axis, distance):
    devices = range(lax.axis_size(axis))
    return lax.ppermute(block, axis, [(i, i + distance) for i in devices if i + distance in devices])


def pack_body(pos_ref, near_ref, other_ref, taps_ref, gains_ref, out_ref):
    odd = lax.rem(pos_ref[0], 2) == 1
    near = near_ref[...].astype(jnp.float32)
    other = other_ref[...].astype(jnp.float32)
    out_ref[0:RIM, :] = jnp.where(odd, near, other)
    out_ref[RIM : 2 * RIM, :] = jnp.where(odd, other, near)
    out_ref[2 * RIM : 2 * RIM + KW, :] = taps_ref[...]
    out_ref[2 * RIM + KW : 2 * RIM + KW + 2, :] = gains_ref[...]
    out_ref[2 * RIM + KW + 2 :, :] = jnp.zeros((7, out_ref.shape[1]), jnp.float32)


def place(dec, blocks, whole_ref, width):
    for offset, block in blocks:
        at = pl.multiple_of((dec ^ offset) * width, width)
        whole_ref[pl.ds(at, width), :] = block[:width, :]


def rounded(value):
    return value.astype(jnp.bfloat16).astype(jnp.float32)


def front_body(
    dec_ref, own_ref, b1_ref, b2_ref, b3_ref, pays_ref, w_hbm, q_ref, kv_ref, resid_ref,
    xall_ref, x_ref, pad_ref, scale_ref, square_ref, whole_ref, turned_ref, norm_ref, pay_ref, w_ref, sem,
):
    width, rows = own_ref.shape
    dec = dec_ref[0]
    fetch = pltpu.make_async_copy(w_hbm, w_ref, sem)
    fetch.start()
    place(dec, [(0, own_ref), (1, b1_ref), (2, b2_ref), (3, b3_ref)], xall_ref, width)
    for n in range(4):
        pay_ref[:, n * width : (n + 1) * width] = pays_ref[n]
    tiles = D // LANES

    def gather_square(f, total):
        at = pl.ds(pl.multiple_of(f * LANES, LANES), LANES)
        x = xall_ref[at, :].astype(jnp.float32)
        return total + jnp.sum((x * x).reshape(LANES // 8, 8, rows), axis=0)

    total = lax.fori_loop(0, tiles, gather_square, jnp.zeros((8, rows), jnp.float32))
    scale = lax.rsqrt(jnp.sum(total, axis=0, keepdims=True) / D + EPS)
    scale_ref[...] = jnp.broadcast_to(scale, (LANES, rows)).T
    rims = pay_ref[0 : 2 * RIM, :]
    rim_scale = lax.rsqrt(jnp.sum(rims * rims, axis=1, keepdims=True) / D + EPS)
    square_ref[...] = jnp.zeros_like(square_ref)
    strip = 64

    def tile(f, carry):
        lanes = pl.ds(pl.multiple_of(f * LANES, LANES), LANES)
        gain = pay_ref[2 * RIM + KW : 2 * RIM + KW + 1, lanes]
        x_ref[...] = xall_ref[lanes, :].astype(jnp.float32).T
        rim = rounded(pay_ref[0 : 2 * RIM, lanes] * rim_scale * gain)
        pad_ref[0:RIM, :] = rim[:RIM]
        pad_ref[RIM + rows : 2 * RIM + rows, :] = rim[RIM:]
        pad_ref[RIM : RIM + rows, :] = rounded(x_ref[...] * scale_ref[...] * gain)
        for t in range(0, rows, strip):
            conv = None
            for b in range(8):
                moved = pad_ref[t + b + 1 : t + b + 1 + strip + 24, :]
                for a in range(4):
                    tap = 8 * a + b
                    if tap < KW:
                        k = pay_ref[2 * RIM + tap : 2 * RIM + tap + 1, lanes]
                        term = moved[8 * a : 8 * a + strip] * k
                        conv = term if conv is None else conv + term
            resid = x_ref[t : t + strip, :] + conv / (1.0 + jnp.exp(-conv))
            whole_ref[f, t : t + strip, :] = resid
            square_ref[t : t + strip, :] += resid * resid

        @pl.when((f * LANES < (dec + 1) * width) & ((f + 1) * LANES > dec * width))
        def _():
            turned_ref[lanes, :] = whole_ref[f].T

        return carry

    lax.fori_loop(0, tiles, tile, 0)
    resid_ref[...] = turned_ref[pl.ds(pl.multiple_of(dec * width, HD), width), :]
    scale2 = lax.rsqrt(jnp.sum(square_ref[...], axis=1, keepdims=True) / D + EPS)
    for f in range(tiles):
        lanes = slice(f * LANES, (f + 1) * LANES)
        gain = pay_ref[2 * RIM + KW + 1 : 2 * RIM + KW + 2, lanes]
        norm_ref[:, lanes] = (whole_ref[f] * scale2 * gain).astype(jnp.bfloat16)
    fetch.wait()
    for third in (1, 2, 0):
        proj = lax.dot_general(
            w_ref[third * width : (third + 1) * width, :],
            norm_ref[...],
            (((1,), (1,)), ((), ())),
            preferred_element_type=jnp.float32,
        ).astype(jnp.bfloat16)
        if third == 0:
            q_ref[...] = proj * jnp.bfloat16(SCALE)
        else:
            kv_ref[(third - 1) * width : third * width, :] = proj


def tdot(left, right):
    return lax.dot_general(left, right, (((0,), (0,)), ((), ())), preferred_element_type=jnp.float32)


def self_body(pos_ref, q_ref, own_ref, beside_ref, beyond_ref, far_ref, out_ref, left_ref):
    width, rows = q_ref.shape
    tile = rows // 2
    pos = pos_ref[0]
    left_ref[...] = jnp.where(lax.rem(pos, 2) == 1, beside_ref[...], beyond_ref[...])
    has_left = pos >= 1
    has_far = pos >= 2
    j = lax.broadcasted_iota(jnp.int32, (tile, tile), 0)
    i = lax.broadcasted_iota(jnp.int32, (tile, tile), 1)
    after = j > i

    def head(h, carry):
        at = pl.ds(pl.multiple_of(h * HD, HD), HD)
        vt = pl.ds(pl.multiple_of(width + h * HD, HD), HD)
        for part in range(2):
            cols = slice(part * tile, (part + 1) * tile)
            q = q_ref[at, cols]
            pieces = [(far_ref, part * tile, (part + 1) * tile, has_far, 1)]
            if part == 0:
                pieces.append((far_ref, tile, rows, has_far, 0))
            pieces.append((left_ref, 0, rows, has_left, 0))
            if part == 1:
                pieces.append((own_ref, 0, tile, None, 0))
            pieces.append((own_ref, part * tile, (part + 1) * tile, None, 2))
            scores = []
            peak = None
            for ref, lo, hi, present, mask in pieces:
                s = tdot(ref[at, lo:hi], q)
                if mask == 1:
                    s = jnp.where(after, s, -FAR)
                elif mask == 2:
                    s = jnp.where(after, -FAR, s)
                top = jnp.max(s, axis=0, keepdims=True)
                if present is not None:
                    top = jnp.where(present, top, -FAR)
                peak = top if peak is None else jnp.maximum(peak, top)
                scores.append(s)
            peak = peak * LOG2E
            total = None
            acc = None
            for (ref, lo, hi, present, mask), s in zip(pieces, scores):
                less = peak if present is None else jnp.where(present, peak, FAR)
                p = jnp.exp2(s * LOG2E - less)
                add = jnp.sum(p, axis=0, keepdims=True)
                total = add if total is None else total + add
                o = jnp.dot(ref[vt, lo:hi], p.astype(jnp.bfloat16), preferred_element_type=jnp.float32)
                acc = o if acc is None else acc + o
            out_ref[at, cols] = (acc / total).astype(jnp.bfloat16)
        return carry

    lax.fori_loop(0, width // HD, head, 0)


def cross_body(pos_ref, q_ref, ends_ref, beside_ref, own_ref, beyond_ref, out_ref):
    width, tokens = q_ref.shape
    rows = own_ref.shape[1]
    first = ends_ref[0:1, :]
    last = ends_ref[1:2, :]
    pos = pos_ref[0]
    refs = (beside_ref, own_ref, beyond_ref)
    places = (pos ^ 1, pos, jnp.where(lax.rem(pos, 2) == 1, pos + 1, pos - 1))
    keeps = []
    for n in range(3):
        kpos = lax.broadcasted_iota(jnp.int32, (rows, tokens), 0) + places[n] * rows
        keeps.append((kpos >= first) & (kpos < last))

    for h in range(width // HD):
        at = slice(h * HD, (h + 1) * HD)
        vt = slice(width + h * HD, width + (h + 1) * HD)
        q = q_ref[at, :] * jnp.bfloat16(SCALE)
        scores = [jnp.where(keep, tdot(ref[at, :], q), -FAR) for ref, keep in zip(refs, keeps)]
        peak = functools.reduce(jnp.maximum, [jnp.max(s, axis=0, keepdims=True) for s in scores]) * LOG2E
        total = None
        acc = None
        for ref, s in zip(refs, scores):
            p = jnp.exp2(s * LOG2E - peak)
            add = jnp.sum(p, axis=0, keepdims=True)
            total = add if total is None else total + add
            o = jnp.dot(ref[vt, :], p.astype(jnp.bfloat16), preferred_element_type=jnp.float32)
            acc = o if acc is None else acc + o
        out_ref[at, :] = (acc / total).astype(jnp.bfloat16)


def out_body(dec_ref, own_ref, b1_ref, b2_ref, b3_ref, w_ref, resid_ref, out_ref, whole_ref):
    width = own_ref.shape[0]
    place(dec_ref[0], [(0, own_ref), (1, b1_ref), (2, b2_ref), (3, b3_ref)], whole_ref, width)
    mixed = jnp.dot(w_ref[...], whole_ref[...], preferred_element_type=jnp.float32)
    out_ref[...] = (resid_ref[...] + mixed).astype(jnp.bfloat16)


def local(frames, queries, align_start, align_end, gain_conv, conv_kernel, gain_attn, w_qkv, w_out):
    bf16, f32 = jnp.bfloat16, jnp.float32
    x = frames.T
    width, rows = x.shape
    tokens = queries.shape[0]
    dec = lax.axis_index("dec").astype(jnp.int32).reshape(1)
    pos = lax.axis_index("ctx").astype(jnp.int32).reshape(1)
    sds = jax.ShapeDtypeStruct

    head, tail = frames[:RIM], frames[rows - RIM :]
    odd = lax.rem(pos[0], 2) == 1
    near = swapped(jnp.where(odd, head, tail), "ctx", 1)
    other = across(jnp.where(odd, tail, head), "ctx")
    b2, b1, b3 = swapped(x, "dec", 2), swapped(x, "dec", 1), swapped(x, "dec", 3)
    pay = call(
        pack_body,
        sds((72, width), f32),
        1,
        (pos, near, other, conv_kernel, jnp.stack([gain_conv, gain_attn])),
        flops=50_000_000_000,
        nbytes=300_000,
    )
    pay = lax.all_gather(pay, "dec", axis=0)
    w_t = jnp.transpose(w_qkv, (1, 2, 0)).reshape(3 * width, D)
    wo_t = w_out.T
    ends = jnp.stack([jnp.repeat(align_start * FB, TB), jnp.repeat(align_end * FB, TB)], 0)
    ends = jnp.concatenate([ends, jnp.zeros((6, tokens), jnp.int32)], axis=0)

    q, kv, resid = call(
        front_body,
        (sds((width, rows), bf16), sds((2 * width, rows), bf16), sds((width, rows), f32)),
        1,
        (dec, x, b1, b2, b3, pay, w_t),
        hbm=1,
        mib=48,
        scratch=[
            pltpu.VMEM((D, rows), bf16),
            pltpu.VMEM((rows, LANES), f32),
            pltpu.VMEM((rows + 3 * RIM, LANES), f32),
            pltpu.VMEM((rows, LANES), f32),
            pltpu.VMEM((rows, LANES), f32),
            pltpu.VMEM((D // LANES, rows, LANES), f32),
            pltpu.VMEM((D, rows), f32),
            pltpu.VMEM((rows, D), bf16),
            pltpu.VMEM((72, D), f32),
            pltpu.VMEM((3 * width, D), bf16),
            pltpu.SemaphoreType.DMA,
        ],
        flops=2 * 3 * width * D * rows,
        nbytes=5_000_000,
    )
    far = shifted(kv, "ctx", 2)
    beyond = across(kv, "ctx")
    beside = swapped(kv, "ctx", 1)
    attn = call(
        self_body,
        sds((width, rows), bf16),
        1,
        (pos, q, kv, beside, beyond, far),
        scratch=[pltpu.VMEM((2 * width, rows), bf16)],
        flops=8 * width * rows * 1280,
        nbytes=2_500_000,
        exps=5 * rows * 1280,
    )
    a2, a1, a3 = swapped(attn, "dec", 2), swapped(attn, "dec", 1), swapped(attn, "dec", 3)
    crossed = call(
        cross_body,
        sds((width, tokens), bf16),
        1,
        (pos, queries.T, ends, beside, kv, beyond),
        flops=4 * width * tokens * 3 * rows,
        nbytes=2_000_000,
        exps=5 * tokens * 3 * rows,
    )
    encoded = call(
        out_body,
        sds((width, rows), bf16),
        1,
        (dec, attn, a1, a2, a3, wo_t, resid),
        scratch=[pltpu.VMEM((D, rows), bf16)],
        flops=2 * width * D * rows,
        nbytes=3_500_000,
    )
    return (encoded.T, crossed.T)


def solution(mesh):
    placed = (
        P("ctx", "dec"),
        P("ctx", "dec"),
        P("ctx"),
        P("ctx"),
        P("dec"),
        P(None, "dec"),
        P("dec"),
        P(None, None, "dec"),
        P(None, "dec"),
    )
    return jax.shard_map(
        local,
        mesh=mesh,
        in_specs=placed,
        out_specs=(P("ctx", "dec"), P("ctx", "dec")),
        check_vma=False,
    )
```

```python
import functools

import jax
import jax.numpy as jnp
from jax import lax
from jax.experimental import pallas as pl
from jax.experimental.pallas import tpu as pltpu
from jax.sharding import PartitionSpec as P

HD = 64
D = 1280
WIN = 1024
FB = 32
TB = 32
KW = 31
HALF = 15
EPS = 1e-06
SCALE = HD ** (-0.5)
LOG2E = 1.4426950408889634
FAR = 1e30
RIM = 16
LANES = 128

VMEM = pl.BlockSpec(memory_space=pltpu.VMEM)
SMEM = pl.BlockSpec(memory_space=pltpu.SMEM)
HBM = pl.BlockSpec(memory_space=pltpu.HBM)


def call(kernel, outs, smem, operands, scratch=(), hbm=0, mib=32, flops=0, nbytes=0, exps=0):
    specs = [SMEM] * smem + [VMEM] * (len(operands) - smem - hbm) + [HBM] * hbm
    return pl.pallas_call(
        kernel,
        out_shape=outs,
        in_specs=specs,
        out_specs=jax.tree.map(lambda _: VMEM, outs),
        scratch_shapes=list(scratch),
        compiler_params=pltpu.CompilerParams(vmem_limit_bytes=mib * 1024 * 1024),
        cost_estimate=pl.CostEstimate(flops=flops, bytes_accessed=nbytes, transcendentals=exps),
    )(*operands)


def swapped(block, axis, bits):
    return lax.ppermute(block, axis, [(i, i ^ bits) for i in range(lax.axis_size(axis))])


def across(block, axis):
    pairs = range(1, lax.axis_size(axis) - 1, 2)
    return lax.ppermute(block, axis, [(i, i + 1) for i in pairs] + [(i + 1, i) for i in pairs])


def behind(block, axis):
    return lax.ppermute(block, axis, [(i + 1, i) for i in range(1, lax.axis_size(axis) - 1, 2)])


def handed(block, axis):
    return lax.ppermute(block, axis, [(i + 1, i) for i in range(0, lax.axis_size(axis), 2)])


def shifted(block, axis, distance):
    devices = range(lax.axis_size(axis))
    return lax.ppermute(block, axis, [(i, i + distance) for i in devices if i + distance in devices])


def copies_body(x_ref, out_ref, sems):
    moves = [pltpu.make_async_copy(x_ref, out_ref.at[n], sems.at[n]) for n in range(4)]
    for move in moves:
        move.start()
    for move in moves:
        move.wait()


def pack_body(pos_ref, near_ref, other_ref, taps_ref, gains_ref, out_ref):
    odd = lax.rem(pos_ref[0], 2) == 1
    near = near_ref[...].astype(jnp.float32)
    other = other_ref[...].astype(jnp.float32)
    out_ref[0:RIM, :] = jnp.where(odd, near, other)
    out_ref[RIM : 2 * RIM, :] = jnp.where(odd, other, near)
    out_ref[2 * RIM : 2 * RIM + KW, :] = taps_ref[...]
    out_ref[2 * RIM + KW : 2 * RIM + KW + 2, :] = gains_ref[...]
    out_ref[2 * RIM + KW + 2 :, :] = jnp.zeros((7, out_ref.shape[1]), jnp.float32)


def rounded(value):
    return value.astype(jnp.bfloat16).astype(jnp.float32)


def front_body(
    dec_ref, xall_ref, pays_ref, w_hbm, q_ref, kv_ref, resid_ref,
    x_ref, pad_ref, scale_ref, square_ref, whole_ref, turned_ref, norm_ref, pay_ref, w_ref, sem,
):
    width, rows = q_ref.shape
    dec = dec_ref[0]
    fetch = pltpu.make_async_copy(w_hbm, w_ref, sem)
    fetch.start()
    for n in range(4):
        pay_ref[:, n * width : (n + 1) * width] = pays_ref[n]
    tiles = D // LANES

    def gather_square(f, total):
        at = pl.ds(pl.multiple_of(f * LANES, LANES), LANES)
        x = xall_ref[at, :].astype(jnp.float32)
        return total + jnp.sum((x * x).reshape(LANES // 8, 8, rows), axis=0)

    total = lax.fori_loop(0, tiles, gather_square, jnp.zeros((8, rows), jnp.float32))
    scale = lax.rsqrt(jnp.sum(total, axis=0, keepdims=True) / D + EPS)
    scale_ref[...] = jnp.broadcast_to(scale, (LANES, rows)).T
    rims = pay_ref[0 : 2 * RIM, :]
    rim_scale = lax.rsqrt(jnp.sum(rims * rims, axis=1, keepdims=True) / D + EPS)
    square_ref[...] = jnp.zeros_like(square_ref)
    strip = 64

    def tile(f, carry):
        lanes = pl.ds(pl.multiple_of(f * LANES, LANES), LANES)
        gain = pay_ref[2 * RIM + KW : 2 * RIM + KW + 1, lanes]
        x_ref[...] = xall_ref[lanes, :].astype(jnp.float32).T
        rim = rounded(pay_ref[0 : 2 * RIM, lanes] * rim_scale * gain)
        pad_ref[0:RIM, :] = rim[:RIM]
        pad_ref[RIM + rows : 2 * RIM + rows, :] = rim[RIM:]
        pad_ref[RIM : RIM + rows, :] = rounded(x_ref[...] * scale_ref[...] * gain)
        for t in range(0, rows, strip):
            conv = None
            for b in range(8):
                moved = pad_ref[t + b + 1 : t + b + 1 + strip + 24, :]
                for a in range(4):
                    tap = 8 * a + b
                    if tap < KW:
                        k = pay_ref[2 * RIM + tap : 2 * RIM + tap + 1, lanes]
                        term = moved[8 * a : 8 * a + strip] * k
                        conv = term if conv is None else conv + term
            resid = x_ref[t : t + strip, :] + conv / (1.0 + jnp.exp(-conv))
            whole_ref[f, t : t + strip, :] = resid
            square_ref[t : t + strip, :] += resid * resid

        @pl.when((f * LANES < (dec + 1) * width) & ((f + 1) * LANES > dec * width))
        def _():
            turned_ref[lanes, :] = whole_ref[f].T

        return carry

    lax.fori_loop(0, tiles, tile, 0)
    resid_ref[...] = turned_ref[pl.ds(pl.multiple_of(dec * width, HD), width), :].astype(jnp.bfloat16)
    scale2 = lax.rsqrt(jnp.sum(square_ref[...], axis=1, keepdims=True) / D + EPS)
    for f in range(tiles):
        lanes = slice(f * LANES, (f + 1) * LANES)
        gain = pay_ref[2 * RIM + KW + 1 : 2 * RIM + KW + 2, lanes]
        norm_ref[:, lanes] = (whole_ref[f] * scale2 * gain).astype(jnp.bfloat16)
    fetch.wait()
    for third in (1, 2, 0):
        proj = lax.dot_general(
            w_ref[third * width : (third + 1) * width, :],
            norm_ref[...],
            (((1,), (1,)), ((), ())),
            preferred_element_type=jnp.float32,
        ).astype(jnp.bfloat16)
        if third == 0:
            q_ref[...] = proj * jnp.bfloat16(SCALE)
        else:
            kv_ref[(third - 1) * width : third * width, :] = proj


def tdot(left, right):
    return lax.dot_general(left, right, (((0,), (0,)), ((), ())), preferred_element_type=jnp.float32)


def attend(kind, present, q_ref, kv_ref, state, put):
    width, rows = q_ref.shape
    tile = rows // 2
    j = lax.broadcasted_iota(jnp.int32, (tile, tile), 0)
    i = lax.broadcasted_iota(jnp.int32, (tile, tile), 1)
    after = j > i
    for h in range(width // HD):
        at = slice(h * HD, (h + 1) * HD)
        vt = slice(width + h * HD, width + (h + 1) * HD)
        for part in range(2):
            cols = slice(part * tile, (part + 1) * tile)
            low, high = (0, tile), (tile, rows)
            if kind == "own":
                pieces = [(low, 2)] if part == 0 else [(low, 0), (high, 2)]
            elif kind == "far":
                pieces = [(low, 1), (high, 0)] if part == 0 else [(high, 1)]
            else:
                pieces = [((0, rows), 0)]
            q = q_ref[at, cols]
            scores = []
            peak = None
            for (lo, hi), mask in pieces:
                s = tdot(kv_ref[at, lo:hi], q)
                if mask == 1:
                    s = jnp.where(after, s, -FAR)
                elif mask == 2:
                    s = jnp.where(after, -FAR, s)
                top = jnp.max(s, axis=0, keepdims=True)
                peak = top if peak is None else jnp.maximum(peak, top)
                scores.append(s)
            peak = peak * LOG2E
            total = None
            acc = None
            if state is not None:
                acc_ref, stat_ref = state
                old = stat_ref[h : h + 1, cols]
                peak = jnp.maximum(jnp.where(present, peak, -FAR), old)
                fade = jnp.exp2(old - peak)
                total = stat_ref[8 + h : 9 + h, cols] * fade
                acc = acc_ref[at, cols] * fade
                less = jnp.where(present, peak, FAR)
            else:
                less = peak
            for ((lo, hi), mask), s in zip(pieces, scores):
                p = jnp.exp2(s * LOG2E - less)
                add = jnp.sum(p, axis=0, keepdims=True)
                total = add if total is None else total + add
                o = jnp.dot(kv_ref[vt, lo:hi], p.astype(jnp.bfloat16), preferred_element_type=jnp.float32)
                acc = o if acc is None else acc + o
            put(h, at, cols, acc, peak, total)


def keep_state(acc_ref, stat_ref):
    def put(h, at, cols, acc, peak, total):
        acc_ref[at, cols] = acc
        stat_ref[h : h + 1, cols] = peak
        stat_ref[8 + h : 9 + h, cols] = total

    return put


def own_body(q_ref, kv_ref, acc_ref, stat_ref):
    attend("own", True, q_ref, kv_ref, None, keep_state(acc_ref, stat_ref))


def far_body(pos_ref, q_ref, far_ref, acc_ref, stat_ref, acc_out, stat_out):
    attend("far", pos_ref[0] >= 2, q_ref, far_ref, (acc_ref, stat_ref), keep_state(acc_out, stat_out))


def left_body(pos_ref, q_ref, beside_ref, passed_ref, acc_ref, stat_ref, out_ref, left_ref):
    pos = pos_ref[0]
    left_ref[...] = jnp.where(lax.rem(pos, 2) == 1, beside_ref[...], passed_ref[...])

    def put(h, at, cols, acc, peak, total):
        out_ref[at, cols] = (acc / total).astype(jnp.bfloat16)

    attend("left", pos >= 1, q_ref, left_ref, (acc_ref, stat_ref), put)


def cross_body(pos_ref, start_ref, end_ref, q_ref, beside_ref, own_ref, passed_ref, ahead_ref, out_ref, other_ref):
    width, tokens = q_ref.shape
    rows = own_ref.shape[1]
    pos = pos_ref[0]
    odd = lax.rem(pos, 2) == 1
    other_ref[...] = jnp.where(odd, ahead_ref[...], passed_ref[...])
    block = lax.broadcasted_iota(jnp.int32, (1, tokens), 1) // TB
    first = jnp.zeros((1, tokens), jnp.int32)
    last = jnp.zeros((1, tokens), jnp.int32)
    for n in range(tokens // TB):
        first = jnp.where(block == n, start_ref[n] * FB, first)
        last = jnp.where(block == n, end_ref[n] * FB, last)
    blocks = (beside_ref, own_ref, other_ref)
    places = (pos ^ 1, pos, jnp.where(odd, pos + 1, pos - 1))
    keeps = []
    for n in range(3):
        kpos = lax.broadcasted_iota(jnp.int32, (rows, tokens), 0) + places[n] * rows
        keeps.append((kpos >= first) & (kpos < last))

    for h in range(width // HD):
        at = slice(h * HD, (h + 1) * HD)
        vt = slice(width + h * HD, width + (h + 1) * HD)
        q = q_ref[at, :] * jnp.bfloat16(SCALE)
        scores = [jnp.where(keep, tdot(ref[at, :], q), -FAR) for ref, keep in zip(blocks, keeps)]
        peak = functools.reduce(jnp.maximum, [jnp.max(s, axis=0, keepdims=True) for s in scores]) * LOG2E
        total = None
        acc = None
        for ref, s in zip(blocks, scores):
            p = jnp.exp2(s * LOG2E - peak)
            add = jnp.sum(p, axis=0, keepdims=True)
            total = add if total is None else total + add
            o = jnp.dot(ref[vt, :], p.astype(jnp.bfloat16), preferred_element_type=jnp.float32)
            acc = o if acc is None else acc + o
        out_ref[at, :] = (acc / total).astype(jnp.bfloat16)


def out_body(dec_ref, b0_ref, b1_ref, b2_ref, b3_ref, w_ref, resid_ref, out_ref, whole_ref):
    width = out_ref.shape[0]
    for n, block in zip((0, 1, 3, 2), (b0_ref, b1_ref, b2_ref, b3_ref)):
        at = pl.multiple_of((dec_ref[0] ^ n) * width, HD)
        whole_ref[pl.ds(at, width), :] = block[...]
    mixed = jnp.dot(w_ref[...], whole_ref[...], preferred_element_type=jnp.float32)
    out_ref[...] = (resid_ref[...].astype(jnp.float32) + mixed).astype(jnp.bfloat16)


def local(frames, queries, align_start, align_end, gain_conv, conv_kernel, gain_attn, w_qkv, w_out):
    bf16, f32 = jnp.bfloat16, jnp.float32
    x = frames.T
    width, rows = x.shape
    tokens = queries.shape[0]
    dec = lax.axis_index("dec").astype(jnp.int32).reshape(1)
    pos = lax.axis_index("ctx").astype(jnp.int32).reshape(1)
    sds = jax.ShapeDtypeStruct

    head, tail = frames[:RIM], frames[rows - RIM :]
    odd = lax.rem(pos[0], 2) == 1
    near = swapped(jnp.where(odd, head, tail), "ctx", 1)
    other = across(jnp.where(odd, tail, head), "ctx")
    copies = pl.pallas_call(
        copies_body,
        out_shape=sds((4, width, rows), bf16),
        in_specs=[VMEM],
        out_specs=HBM,
        scratch_shapes=[pltpu.SemaphoreType.DMA((4,))],
        cost_estimate=pl.CostEstimate(flops=0, bytes_accessed=2_000_000, transcendentals=0),
    )(x)
    x_all = lax.all_to_all(copies, "dec", 0, 0).reshape(D, rows)
    pay = call(
        pack_body,
        sds((72, width), f32),
        1,
        (pos, near, other, conv_kernel, jnp.stack([gain_conv, gain_attn])),
        flops=1_000_000,
        nbytes=300_000,
    )
    pays = lax.all_gather(pay, "dec", axis=0)
    w_t = jnp.transpose(w_qkv, (1, 2, 0)).reshape(3 * width, D)
    wo_t = w_out.T
    q, kv, resid = call(
        front_body,
        (sds((width, rows), bf16), sds((2 * width, rows), bf16), sds((width, rows), bf16)),
        1,
        (dec, x_all, pays, w_t),
        hbm=1,
        mib=50,
        scratch=[
            pltpu.VMEM((rows, LANES), f32),
            pltpu.VMEM((rows + 3 * RIM, LANES), f32),
            pltpu.VMEM((rows, LANES), f32),
            pltpu.VMEM((rows, LANES), f32),
            pltpu.VMEM((D // LANES, rows, LANES), f32),
            pltpu.VMEM((D, rows), f32),
            pltpu.VMEM((rows, D), bf16),
            pltpu.VMEM((72, D), f32),
            pltpu.VMEM((3 * width, D), bf16),
            pltpu.SemaphoreType.DMA,
        ],
        flops=2 * 3 * width * D * rows,
        nbytes=5_000_000,
    )
    beside = swapped(kv, "ctx", 1)
    ahead = behind(kv, "ctx")
    far = shifted(kv, "ctx", 2)
    state = (sds((width, rows), f32), sds((16, rows), f32))
    work = dict(flops=4 * width * rows * rows, nbytes=2_500_000, exps=5 * rows * 512)
    acc, stat = call(own_body, state, 0, (q, kv), **work)
    beside, ahead, far, acc, stat = lax.optimization_barrier((beside, ahead, far, acc, stat))
    passed = handed(far, "ctx")
    acc, stat = call(far_body, state, 1, (pos, q, far, acc, stat), **work)
    attn = call(
        left_body,
        sds((width, rows), bf16),
        1,
        (pos, q, beside, passed, acc, stat),
        scratch=[pltpu.VMEM((2 * width, rows), bf16)],
        **work,
    )
    whole = [attn] + [swapped(attn, "dec", bits) for bits in (1, 3, 2)]
    attn_q, _ = lax.optimization_barrier((queries.T, attn))
    crossed = call(
        cross_body,
        sds((width, tokens), bf16),
        3,
        (pos, align_start, align_end, attn_q, beside, kv, passed, ahead),
        scratch=[pltpu.VMEM((2 * width, rows), bf16)],
        flops=4 * width * tokens * 3 * rows,
        nbytes=2_000_000,
        exps=5 * tokens * 3 * rows,
    )
    encoded = call(
        out_body,
        sds((width, rows), bf16),
        1,
        (dec, *whole, wo_t, resid),
        scratch=[pltpu.VMEM((D, rows), bf16)],
        flops=2 * width * D * rows,
        nbytes=3_500_000,
    )
    return (encoded.T, crossed.T)


def solution(mesh):
    placed = (
        P("ctx", "dec"),
        P("ctx", "dec"),
        P("ctx"),
        P("ctx"),
        P("dec"),
        P(None, "dec"),
        P("dec"),
        P(None, None, "dec"),
        P(None, "dec"),
    )
    return jax.shard_map(
        local,
        mesh=mesh,
        in_specs=placed,
        out_specs=(P("ctx", "dec"), P("ctx", "dec")),
        check_vma=False,
    )
```

```python
import functools

import jax
import jax.numpy as jnp
from jax import lax
from jax.experimental import pallas as pl
from jax.experimental.pallas import tpu as pltpu
from jax.sharding import PartitionSpec as P

HD = 64
D = 1280
WIN = 1024
FB = 32
TB = 32
KW = 31
HALF = 15
EPS = 1e-06
SCALE = HD ** (-0.5)
LOG2E = 1.4426950408889634
FAR = 1e30
RIM = 16
LANES = 128

VMEM = pl.BlockSpec(memory_space=pltpu.VMEM)
SMEM = pl.BlockSpec(memory_space=pltpu.SMEM)
HBM = pl.BlockSpec(memory_space=pltpu.HBM)


def call(kernel, outs, smem, operands, scratch=(), hbm=0, mib=32, flops=0, nbytes=0, exps=0):
    specs = [SMEM] * smem + [VMEM] * (len(operands) - smem - hbm) + [HBM] * hbm
    return pl.pallas_call(
        kernel,
        out_shape=outs,
        in_specs=specs,
        out_specs=jax.tree.map(lambda _: VMEM, outs),
        scratch_shapes=list(scratch),
        compiler_params=pltpu.CompilerParams(vmem_limit_bytes=mib * 1024 * 1024),
        cost_estimate=pl.CostEstimate(flops=flops, bytes_accessed=nbytes, transcendentals=exps),
    )(*operands)


def swapped(block, axis, bits):
    return lax.ppermute(block, axis, [(i, i ^ bits) for i in range(lax.axis_size(axis))])


def across(block, axis):
    pairs = range(1, lax.axis_size(axis) - 1, 2)
    return lax.ppermute(block, axis, [(i, i + 1) for i in pairs] + [(i + 1, i) for i in pairs])


def behind(block, axis):
    return lax.ppermute(block, axis, [(i + 1, i) for i in range(1, lax.axis_size(axis) - 1, 2)])


def handed(block, axis):
    return lax.ppermute(block, axis, [(i + 1, i) for i in range(0, lax.axis_size(axis), 2)])


def shifted(block, axis, distance):
    devices = range(lax.axis_size(axis))
    return lax.ppermute(block, axis, [(i, i + distance) for i in devices if i + distance in devices])


def copies_body(x_ref, out_ref):
    for n in range(4):
        out_ref[n] = x_ref[...]


def pack_body(pos_ref, near_ref, other_ref, taps_ref, gains_ref, out_ref):
    odd = lax.rem(pos_ref[0], 2) == 1
    near = near_ref[...].astype(jnp.float32)
    other = other_ref[...].astype(jnp.float32)
    out_ref[0:RIM, :] = jnp.where(odd, near, other)
    out_ref[RIM : 2 * RIM, :] = jnp.where(odd, other, near)
    out_ref[2 * RIM : 2 * RIM + KW, :] = taps_ref[...]
    out_ref[2 * RIM + KW : 2 * RIM + KW + 2, :] = gains_ref[...]
    out_ref[2 * RIM + KW + 2 :, :] = jnp.zeros((7, out_ref.shape[1]), jnp.float32)


def rounded(value):
    return value.astype(jnp.bfloat16).astype(jnp.float32)


def front_body(
    dec_ref, xall_ref, pays_ref, w_hbm, q_ref, kv_ref, resid_ref,
    x0_ref, pad0_ref, x1_ref, pad1_ref, scale_ref, square_ref, whole_ref, turned_ref, norm_ref, pay_ref, w_ref, sem,
):
    width, rows = q_ref.shape
    dec = dec_ref[0]
    fetch = pltpu.make_async_copy(w_hbm, w_ref, sem)
    fetch.start()
    for n in range(4):
        pay_ref[:, n * width : (n + 1) * width] = pays_ref[n]
    tiles = D // LANES

    def gather_square(f, total):
        at = pl.ds(pl.multiple_of(f * LANES, LANES), LANES)
        x = xall_ref[at, :].astype(jnp.float32)
        return total + jnp.sum((x * x).reshape(LANES // 8, 8, rows), axis=0)

    total = lax.fori_loop(0, tiles, gather_square, jnp.zeros((8, rows), jnp.float32))
    scale = lax.rsqrt(jnp.sum(total, axis=0, keepdims=True) / D + EPS)
    scale_ref[...] = jnp.broadcast_to(scale, (LANES, rows)).T
    rims = pay_ref[0 : 2 * RIM, :]
    rim_scale = lax.rsqrt(jnp.sum(rims * rims, axis=1, keepdims=True) / D + EPS)
    square_ref[...] = jnp.zeros_like(square_ref)
    strip = 64

    def prepare(f, x_ref, pad_ref):
        lanes = pl.ds(pl.multiple_of(f * LANES, LANES), LANES)
        gain = pay_ref[2 * RIM + KW : 2 * RIM + KW + 1, lanes]
        x_ref[...] = xall_ref[lanes, :].astype(jnp.float32).T
        rim = rounded(pay_ref[0 : 2 * RIM, lanes] * rim_scale * gain)
        pad_ref[0:RIM, :] = rim[:RIM]
        pad_ref[RIM + rows : 2 * RIM + rows, :] = rim[RIM:]
        pad_ref[RIM : RIM + rows, :] = rounded(x_ref[...] * scale_ref[...] * gain)

    def convolve(f, x_ref, pad_ref):
        lanes = pl.ds(pl.multiple_of(f * LANES, LANES), LANES)
        for t in range(0, rows, strip):
            conv = None
            for b in range(8):
                moved = pad_ref[t + b + 1 : t + b + 1 + strip + 24, :]
                for a in range(4):
                    tap = 8 * a + b
                    if tap < KW:
                        k = pay_ref[2 * RIM + tap : 2 * RIM + tap + 1, lanes]
                        term = moved[8 * a : 8 * a + strip] * k
                        conv = term if conv is None else conv + term
            resid = x_ref[t : t + strip, :] + conv / (1.0 + jnp.exp(-conv))
            whole_ref[f, t : t + strip, :] = resid
            square_ref[t : t + strip, :] += resid * resid

    def two_tiles(n, carry):
        prepare(2 * n + 1, x1_ref, pad1_ref)
        convolve(2 * n, x0_ref, pad0_ref)
        prepare(jnp.minimum(2 * n + 2, tiles - 1), x0_ref, pad0_ref)
        convolve(2 * n + 1, x1_ref, pad1_ref)
        return carry

    prepare(0, x0_ref, pad0_ref)
    lax.fori_loop(0, tiles // 2, two_tiles, 0)
    begin = (dec * width) // LANES
    for n in range(3):
        turned_ref[n * LANES : (n + 1) * LANES, :] = whole_ref[begin + n].T
    offset = pl.multiple_of(dec * width - begin * LANES, HD)
    resid_ref[...] = turned_ref[pl.ds(offset, width), :].astype(jnp.bfloat16)
    scale2 = lax.rsqrt(jnp.sum(square_ref[...], axis=1, keepdims=True) / D + EPS)
    for f in range(tiles):
        lanes = slice(f * LANES, (f + 1) * LANES)
        gain = pay_ref[2 * RIM + KW + 1 : 2 * RIM + KW + 2, lanes]
        norm_ref[:, lanes] = (whole_ref[f] * scale2 * gain).astype(jnp.bfloat16)
    fetch.wait()
    for third in (1, 2, 0):
        proj = lax.dot_general(
            w_ref[third * width : (third + 1) * width, :],
            norm_ref[...],
            (((1,), (1,)), ((), ())),
            preferred_element_type=jnp.float32,
        ).astype(jnp.bfloat16)
        if third == 0:
            q_ref[...] = proj * jnp.bfloat16(SCALE)
        else:
            kv_ref[(third - 1) * width : third * width, :] = proj


def tdot(left, right):
    return lax.dot_general(left, right, (((0,), (0,)), ((), ())), preferred_element_type=jnp.float32)


def attend(kind, present, q_ref, kv_ref, state, put):
    width, rows = q_ref.shape
    half = rows // 2
    j = lax.broadcasted_iota(jnp.int32, (half, rows), 0)
    i = lax.broadcasted_iota(jnp.int32, (half, rows), 1)
    if kind == "own":
        pieces = [((0, half), (0, rows), j > i), ((half, rows), (half, rows), (j > i)[:, :half])]
    elif kind == "far":
        pieces = [((half, rows), (0, rows), j + half <= i), ((0, half), (0, half), (j <= i)[:, :half])]
    else:
        pieces = [((0, rows), (0, rows), None)]
    for h in range(width // HD):
        at = slice(h * HD, (h + 1) * HD)
        vt = slice(width + h * HD, width + (h + 1) * HD)
        scores = []
        peaks = [None, None]
        for (lo, hi), (first, last), drop in pieces:
            s = tdot(kv_ref[at, lo:hi], q_ref[at, first:last])
            if drop is not None:
                s = jnp.where(drop, -FAR, s)
            top = jnp.max(s, axis=0, keepdims=True)
            for side in range(2):
                if first <= side * half < last:
                    part = top[:, side * half - first : side * half - first + half]
                    peaks[side] = part if peaks[side] is None else jnp.maximum(peaks[side], part)
            scores.append(s)
        peak = jnp.concatenate(peaks, axis=1) * LOG2E
        if state is not None:
            acc_ref, stat_ref = state
            old = stat_ref[h : h + 1, :]
            peak = jnp.maximum(jnp.where(present, peak, -FAR), old)
            fade = jnp.exp2(old - peak)
            total = stat_ref[8 + h : 9 + h, :] * fade
            acc = acc_ref[at, :] * fade
            less = jnp.where(present, peak, FAR)
            totals = [total[:, :half], total[:, half:]]
            accs = [acc[:, :half], acc[:, half:]]
        else:
            less = peak
            totals = [None, None]
            accs = [None, None]
        for ((lo, hi), (first, last), _), s in zip(pieces, scores):
            p = jnp.exp2(s * LOG2E - less[:, first:last])
            add = jnp.sum(p, axis=0, keepdims=True)
            o = jnp.dot(kv_ref[vt, lo:hi], p.astype(jnp.bfloat16), preferred_element_type=jnp.float32)
            for side in range(2):
                if first <= side * half < last:
                    cut = slice(side * half - first, side * half - first + half)
                    totals[side] = add[:, cut] if totals[side] is None else totals[side] + add[:, cut]
                    accs[side] = o[:, cut] if accs[side] is None else accs[side] + o[:, cut]
        for side in range(2):
            cols = slice(side * half, (side + 1) * half)
            put(h, at, cols, accs[side], peak[:, cols], totals[side])


def keep_state(acc_ref, stat_ref):
    def put(h, at, cols, acc, peak, total):
        acc_ref[at, cols] = acc
        stat_ref[h : h + 1, cols] = peak
        stat_ref[8 + h : 9 + h, cols] = total

    return put


def own_body(q_ref, kv_ref, acc_ref, stat_ref):
    attend("own", True, q_ref, kv_ref, None, keep_state(acc_ref, stat_ref))


def far_body(pos_ref, q_ref, far_ref, acc_ref, stat_ref, acc_out, stat_out):
    attend("far", pos_ref[0] >= 2, q_ref, far_ref, (acc_ref, stat_ref), keep_state(acc_out, stat_out))


def left_body(pos_ref, q_ref, beside_ref, passed_ref, acc_ref, stat_ref, out_ref, left_ref):
    pos = pos_ref[0]
    left_ref[...] = jnp.where(lax.rem(pos, 2) == 1, beside_ref[...], passed_ref[...])

    def put(h, at, cols, acc, peak, total):
        out_ref[at, cols] = (acc / total).astype(jnp.bfloat16)

    attend("left", pos >= 1, q_ref, left_ref, (acc_ref, stat_ref), put)


def cross_body(pos_ref, start_ref, end_ref, q_ref, beside_ref, own_ref, passed_ref, ahead_ref, out_ref, other_ref):
    width, tokens = q_ref.shape
    rows = own_ref.shape[1]
    pos = pos_ref[0]
    odd = lax.rem(pos, 2) == 1
    other_ref[...] = jnp.where(odd, ahead_ref[...], passed_ref[...])
    block = lax.broadcasted_iota(jnp.int32, (1, tokens), 1) // TB
    first = jnp.zeros((1, tokens), jnp.int32)
    last = jnp.zeros((1, tokens), jnp.int32)
    for n in range(tokens // TB):
        first = jnp.where(block == n, start_ref[n] * FB, first)
        last = jnp.where(block == n, end_ref[n] * FB, last)
    blocks = (beside_ref, own_ref, other_ref)
    places = (pos ^ 1, pos, jnp.where(odd, pos + 1, pos - 1))
    keeps = []
    for n in range(3):
        kpos = lax.broadcasted_iota(jnp.int32, (rows, tokens), 0) + places[n] * rows
        keeps.append((kpos >= first) & (kpos < last))

    for h in range(width // HD):
        at = slice(h * HD, (h + 1) * HD)
        vt = slice(width + h * HD, width + (h + 1) * HD)
        q = q_ref[at, :] * jnp.bfloat16(SCALE)
        scores = [jnp.where(keep, tdot(ref[at, :], q), -FAR) for ref, keep in zip(blocks, keeps)]
        peak = functools.reduce(jnp.maximum, [jnp.max(s, axis=0, keepdims=True) for s in scores]) * LOG2E
        total = None
        acc = None
        for ref, s in zip(blocks, scores):
            p = jnp.exp2(s * LOG2E - peak)
            add = jnp.sum(p, axis=0, keepdims=True)
            total = add if total is None else total + add
            o = jnp.dot(ref[vt, :], p.astype(jnp.bfloat16), preferred_element_type=jnp.float32)
            acc = o if acc is None else acc + o
        out_ref[at, :] = (acc / total).astype(jnp.bfloat16)


def out_body(dec_ref, b0_ref, b1_ref, b2_ref, b3_ref, w_ref, resid_ref, out_ref, whole_ref):
    width = out_ref.shape[0]
    for n, block in zip((0, 1, 3, 2), (b0_ref, b1_ref, b2_ref, b3_ref)):
        at = pl.multiple_of((dec_ref[0] ^ n) * width, HD)
        whole_ref[pl.ds(at, width), :] = block[...]
    mixed = jnp.dot(w_ref[...], whole_ref[...], preferred_element_type=jnp.float32)
    out_ref[...] = (resid_ref[...].astype(jnp.float32) + mixed).astype(jnp.bfloat16)


def local(frames, queries, align_start, align_end, gain_conv, conv_kernel, gain_attn, w_qkv, w_out):
    bf16, f32 = jnp.bfloat16, jnp.float32
    x = frames.T
    width, rows = x.shape
    tokens = queries.shape[0]
    dec = lax.axis_index("dec").astype(jnp.int32).reshape(1)
    pos = lax.axis_index("ctx").astype(jnp.int32).reshape(1)
    sds = jax.ShapeDtypeStruct

    head, tail = frames[:RIM], frames[rows - RIM :]
    odd = lax.rem(pos[0], 2) == 1
    near = swapped(jnp.where(odd, head, tail), "ctx", 1)
    other = across(jnp.where(odd, tail, head), "ctx")
    copies = call(copies_body, sds((4, width, rows), bf16), 0, (x,), nbytes=2_000_000)
    x_all = lax.all_to_all(copies, "dec", 0, 0).reshape(D, rows)
    pay = call(
        pack_body,
        sds((72, width), f32),
        1,
        (pos, near, other, conv_kernel, jnp.stack([gain_conv, gain_attn])),
        flops=1_000_000,
        nbytes=300_000,
    )
    pays = lax.all_gather(pay, "dec", axis=0)
    w_t = jnp.transpose(w_qkv, (1, 2, 0)).reshape(3 * width, D)
    wo_t = w_out.T
    q, kv, resid = call(
        front_body,
        (sds((width, rows), bf16), sds((2 * width, rows), bf16), sds((width, rows), bf16)),
        1,
        (dec, x_all, pays, w_t),
        hbm=1,
        mib=50,
        scratch=[
            pltpu.VMEM((rows, LANES), f32),
            pltpu.VMEM((rows + 3 * RIM, LANES), f32),
            pltpu.VMEM((rows, LANES), f32),
            pltpu.VMEM((rows + 3 * RIM, LANES), f32),
            pltpu.VMEM((rows, LANES), f32),
            pltpu.VMEM((rows, LANES), f32),
            pltpu.VMEM((D // LANES, rows, LANES), f32),
            pltpu.VMEM((3 * LANES, rows), f32),
            pltpu.VMEM((rows, D), bf16),
            pltpu.VMEM((72, D), f32),
            pltpu.VMEM((3 * width, D), bf16),
            pltpu.SemaphoreType.DMA,
        ],
        flops=2 * 3 * width * D * rows,
        nbytes=5_000_000,
    )
    beside = swapped(kv, "ctx", 1)
    ahead = behind(kv, "ctx")
    far = shifted(kv, "ctx", 2)
    state = (sds((width, rows), f32), sds((16, rows), f32))
    work = dict(flops=4 * width * rows * rows, nbytes=2_500_000, exps=5 * rows * 512)
    acc, stat = call(own_body, state, 0, (q, kv), **work)
    beside, ahead, far, acc, stat = lax.optimization_barrier((beside, ahead, far, acc, stat))
    passed = handed(far, "ctx")
    acc, stat = call(far_body, state, 1, (pos, q, far, acc, stat), **work)
    attn = call(
        left_body,
        sds((width, rows), bf16),
        1,
        (pos, q, beside, passed, acc, stat),
        scratch=[pltpu.VMEM((2 * width, rows), bf16)],
        **work,
    )
    whole = [attn] + [swapped(attn, "dec", bits) for bits in (1, 3, 2)]
    attn_q, _ = lax.optimization_barrier((queries.T, attn))
    crossed = call(
        cross_body,
        sds((width, tokens), bf16),
        3,
        (pos, align_start, align_end, attn_q, beside, kv, passed, ahead),
        scratch=[pltpu.VMEM((2 * width, rows), bf16)],
        flops=4 * width * tokens * 3 * rows,
        nbytes=2_000_000,
        exps=5 * tokens * 3 * rows,
    )
    encoded = call(
        out_body,
        sds((width, rows), bf16),
        1,
        (dec, *whole, wo_t, resid),
        scratch=[pltpu.VMEM((D, rows), bf16)],
        flops=2 * width * D * rows,
        nbytes=3_500_000,
    )
    return (encoded.T, crossed.T)


def solution(mesh):
    placed = (
        P("ctx", "dec"),
        P("ctx", "dec"),
        P("ctx"),
        P("ctx"),
        P("dec"),
        P(None, "dec"),
        P("dec"),
        P(None, None, "dec"),
        P(None, "dec"),
    )
    return jax.shard_map(
        local,
        mesh=mesh,
        in_specs=placed,
        out_specs=(P("ctx", "dec"), P("ctx", "dec")),
        check_vma=False,
    )
```
